32 devices in a mesh: cells: 8 (over y, x, core), stations: 4 (over z).
Axes of the slice: x: 2, y: 2, z: 4, core: 2. Of those that a mesh axis runs over, the one named last changes fastest.
Arguments:
- probes: bfloat16 [16, 32768], P(None, 'cells'), may hold values from -6 to 6
- reg_weight: float32 [32768], P('cells'), may hold values from 0.1 to 1
- cell_plan: int32 [2, 32768], P(None, 'cells'), may hold values from 0 to 255
- cell_depth: int32 [32768], P('cells'), may hold values from 0 to 15, as said below
- station_index: int32 [2, 16384], P(None, 'stations'), may hold values from 0 to 65535, as said below
- station_weight: float32 [16384], P('stations'), may hold values from 0.5 to 2
Outputs:
- basis: float32 [16, 32768], P(None, ('cells', 'stations'))
- factor: float32 [16, 16], replicated
The draws below stay inside these ranges and needn't reach their ends.
Inputs may be any that keep to these rules, and one draw needn't show every extreme that they name: `cell_plan`: east and north cell indices of a grid of 256 by 256 columns. `cell_depth`: depth indices of 16 layers. `station_index`: east and north station positions in 1/256ths of a cell width, over the same area as the cells' grid.
All inputs are finite; a program needn't handle non-finite values.
Results may differ from the reference program's by a relative error of at most 0.00065.
Values may be sent and summed in bfloat16 or wider, within the bound.
A program may use at most 64 MiB of HBM per device.

```python
import math
import jax
import jax.numpy as jnp
from jax import lax

K = 16
CELLS = 32768
STATIONS = 16384


def draw_station_index(key, part):
    raw_points = jax.random.randint(key, (2, STATIONS), 0, 65536, dtype=jnp.int32)
    highest = jnp.max(raw_points, axis=1, keepdims=True)
    return raw_points + (65535 - highest)


def draw_cell_depth(key, part):
    positions = jnp.arange(CELLS, dtype=jnp.int32)
    layer_base = 15 - positions * 16 // CELLS
    jitter_steps = jax.random.randint(jax.random.fold_in(key, 7), (CELLS,), -2, 3, dtype=jnp.int32)
    return jnp.clip(layer_base + jitter_steps, 0, 15).astype(jnp.int32)


def set_ends(drawn, stream_key, smallest, largest):
    shape = drawn.shape
    place = [jax.random.randint(jax.random.fold_in(stream_key, axis), (), 0, shape[axis]) for axis in range(len(shape))]
    drawn = drawn.at[tuple(place)].set(smallest)
    longest = shape.index(max(shape))
    place[longest] = (place[longest] + 1) % shape[longest]
    return drawn.at[tuple(place)].set(largest)


def block_levels(rng, extent, cuts, low, high):
    factor_of, own = 1.0, jax.random.fold_in(rng, 6)
    for position, parts in cuts:
        steps = jnp.exp(jax.random.uniform(jax.random.fold_in(own, position), (parts,), jnp.float32, low / len(cuts), high / len(cuts)))
        factor_of = factor_of * jnp.repeat(steps, extent[position] // parts).reshape([-1 if axis == position else 1 for axis in range(len(extent))])
    return factor_of


def normal_values(key, extent, width, limit, cuts=(), kind=jnp.bfloat16):
    entries = width * jax.random.normal(key, extent, jnp.float32)
    if cuts:
        entries = entries * block_levels(key, extent, cuts, -0.22, 0.18)
    return jnp.clip(entries, -limit, limit).astype(kind)


def setup_inputs(seed: int = 0) -> dict:
    streams_of = jax.random.split(jax.random.key(seed), 7)
    probes = normal_values(streams_of[0], (K, CELLS), 1.0, 6.0, ((1, 8),))
    reg_weight = jnp.clip(jnp.exp(math.log(1.0) - 2.3025851 * jax.random.uniform(streams_of[1], (CELLS,), jnp.float32) ** block_levels(streams_of[1], (CELLS,), ((0, 8),), -0.2, 0.2)), 0.1, 1.0)
    cell_plan = set_ends(jax.random.randint(streams_of[2], (2, CELLS), 0, 256), jax.random.fold_in(streams_of[2], 1), 0, 255).astype(jnp.int32)
    cell_depth = draw_cell_depth(jax.random.fold_in(streams_of[6], 71), 0)
    station_index = draw_station_index(jax.random.fold_in(streams_of[6], 71), 0)
    station_weight = jnp.clip(jnp.exp(math.log(2.0) - 1.3862944 * jax.random.uniform(streams_of[5], (STATIONS,), jnp.float32) ** block_levels(streams_of[5], (STATIONS,), ((0, 4),), -0.2, 0.2)), 0.5, 2.0)
    return dict(probes=probes, reg_weight=reg_weight, cell_plan=cell_plan, cell_depth=cell_depth, station_index=station_index, station_weight=station_weight)


GRAVITY = 2.0
JITTER = 1e-06
SUBSTEP = 0.00390625

def cell_points(cell_plan, cell_depth):
    cell_east = cell_plan[0].astype(jnp.float32) + 0.5
    cell_north = cell_plan[1].astype(jnp.float32) + 0.5
    cell_down = cell_depth.astype(jnp.float32) + 1.0
    return (cell_east, cell_north, cell_down)

def sensitivity(st_east, st_north, cell_east, cell_north, cell_down):
    d_east = cell_east[None, :] - st_east[:, None]
    d_north = cell_north[None, :] - st_north[:, None]
    distance = d_east * d_east + d_north * d_north + cell_down[None, :] * cell_down[None, :]
    inverse = lax.rsqrt(distance)
    return (GRAVITY * cell_down[None, :] * inverse * inverse * inverse).astype(jnp.bfloat16)

def widened(sens_tile):
    return lax.optimization_barrier(sens_tile).astype(jnp.float32)

def reference(probes, reg_weight, cell_plan, cell_depth, station_index, station_weight):
    cell_east, cell_north, cell_down = cell_points(cell_plan, cell_depth)
    st_east = station_index[0].astype(jnp.float32) * SUBSTEP
    st_north = station_index[1].astype(jnp.float32) * SUBSTEP
    ref_block = math.gcd(STATIONS, 64)
    block_total = STATIONS // ref_block
    probe_wide = probes.astype(jnp.float32)

    def forward_block(turn_index):
        start_at = turn_index * ref_block
        sens_tile = widened(sensitivity(lax.dynamic_slice_in_dim(st_east, start_at, ref_block), lax.dynamic_slice_in_dim(st_north, start_at, ref_block), cell_east, cell_north, cell_down))
        return lax.dot_general(probe_wide.astype(jnp.float32), sens_tile.astype(jnp.float32), (((1,), (1,)), ((), ())), preferred_element_type=jnp.float32)
    stacked = lax.map(forward_block, jnp.arange(block_total, dtype=jnp.int32))
    station_field = jnp.transpose(stacked, (1, 0, 2)).reshape(K, STATIONS)
    weighted = (station_weight[None, :] * station_weight[None, :] * station_field).astype(jnp.bfloat16)
    weighted_wide = weighted.astype(jnp.float32)

    def backward_block(turn_index, running):
        start_at = turn_index * ref_block
        sens_tile = widened(sensitivity(lax.dynamic_slice_in_dim(st_east, start_at, ref_block), lax.dynamic_slice_in_dim(st_north, start_at, ref_block), cell_east, cell_north, cell_down))
        segment = lax.dynamic_slice_in_dim(weighted_wide, start_at, ref_block, 1)
        return running + jnp.dot(segment.astype(jnp.float32), sens_tile.astype(jnp.float32), preferred_element_type=jnp.float32)
    hess_image = lax.fori_loop(0, block_total, backward_block, jnp.zeros((K, CELLS), jnp.float32))
    hess_image = hess_image + reg_weight[None, :] * probe_wide
    gram_matrix = jnp.dot(hess_image.astype(jnp.float32), hess_image.T.astype(jnp.float32), precision=lax.Precision.HIGHEST, preferred_element_type=jnp.float32) / CELLS
    gram_matrix = gram_matrix + JITTER * jnp.eye(K, dtype=jnp.float32)
    lower_factor = jnp.linalg.cholesky(gram_matrix)
    basis_rows = jax.scipy.linalg.solve_triangular(lower_factor, hess_image, lower=True)
    return (basis_rows, lower_factor)
```

```python
import functools

import jax
import jax.numpy as jnp
from jax import lax
from jax.experimental import pallas as pl
from jax.experimental.pallas import tpu as pltpu
from jax.sharding import PartitionSpec as P

JITTER = 1e-06
MESH = pl.DeviceIdType.MESH
F32 = jnp.float32
BF16 = jnp.bfloat16
TILE = 256
FEATURES = 16


def matmul(left, right):
    return jnp.dot(left, right, preferred_element_type=F32)


def matmul_nt(left, right, precision=None):
    return lax.dot_general(
        left, right, (((1,), (1,)), ((), ())), precision=precision, preferred_element_type=F32
    )


def cell_features(plan_ref, depth_ref):
    east = plan_ref[0:1, :] - 128
    north = plan_ref[1:2, :] - 128
    down = depth_ref[...] + 1
    square = east * east + north * north + down * down
    high = (square >> 8) << 8
    low = square & 255
    one = jnp.ones_like(square)
    zero = jnp.zeros_like(square)
    rows = [high, low, one, one, east, north, zero, zero]
    rows += [east, north, one, one, one, zero, zero, zero]
    return jnp.concatenate([row.astype(F32) for row in rows], axis=0)


def station_features(index_ref):
    east, north = index_ref[0:1, :], index_ref[1:2, :]
    whole_e, whole_n = (east >> 8) - 128, (north >> 8) - 128
    part_e, part_n = (east & 255) - 128, (north & 255) - 128
    square = whole_e * whole_e + whole_n * whole_n
    cross = 512 * (whole_e * part_e + whole_n * part_n) + part_e * part_e + part_n * part_n
    one = jnp.ones_like(square).astype(F32)
    zero = jnp.zeros_like(one)
    rows = [
        one,
        one,
        ((square >> 8) << 8).astype(F32),
        (square & 255).astype(F32),
        (-2 * whole_e).astype(F32),
        (-2 * whole_n).astype(F32),
        zero,
        zero,
        part_e.astype(F32) * (-2.0 / 256),
        part_n.astype(F32) * (-2.0 / 256),
        (cross >> 16).astype(F32),
        ((cross >> 8) & 255).astype(F32) * (1.0 / 256),
        (cross & 255).astype(F32) * (1.0 / 65536),
        zero,
        zero,
        zero,
    ]
    return jnp.concatenate(rows, axis=0)


def kernel(
    n_cells,
    n_stations,
    probes_ref,
    reg_ref,
    plan_ref,
    depth_ref,
    index_ref,
    weight_ref,
    basis_ref,
    factor_ref,
    sens,
    cell_feat,
    station_feat,
    scale,
    field_out,
    field_in,
    weighted,
    image_out,
    image_in,
    gram_s,
    gram_c,
    field_send,
    field_recv,
    weighted_send,
    weighted_recv,
    image_send,
    image_recv,
    gs_send,
    gs_recv,
    gc_send,
    gc_recv,
):
    k_rows, cells = probes_ref.shape
    stations = index_ref.shape[1]
    own = stations // n_cells
    quarter = cells // n_stations
    block = max(own, 512)
    block_owners = block // own
    blocks = stations // block
    me_c = lax.axis_index("cells")
    me_s = lax.axis_index("stations")

    def peer_c(step):
        return lax.rem(me_c + step, n_cells)

    def peer_s(step):
        return lax.rem(me_s + step, n_stations)

    barrier = pltpu.get_barrier_semaphore()

    def greet_c(step, carry):
        pl.semaphore_signal(barrier, inc=1, device_id={"cells": peer_c(step)}, device_id_type=MESH)
        return carry

    lax.fori_loop(1, n_cells, greet_c, 0)
    for step in range(1, n_stations):
        pl.semaphore_signal(
            barrier, inc=1, device_id={"stations": peer_s(step)}, device_id_type=MESH
        )

    def field_copy(dest):
        return pltpu.make_async_remote_copy(
            src_ref=field_out.at[dest],
            dst_ref=field_in.at[me_c],
            send_sem=field_send.at[dest],
            recv_sem=field_recv.at[me_c],
            device_id={"cells": dest},
            device_id_type=MESH,
        )

    def field_arrival(source):
        return pltpu.make_async_remote_copy(
            src_ref=field_out.at[source],
            dst_ref=field_in.at[source],
            send_sem=field_send.at[source],
            recv_sem=field_recv.at[source],
            device_id={"cells": source},
            device_id_type=MESH,
        )

    def weighted_copy(dest, source):
        return pltpu.make_async_remote_copy(
            src_ref=weighted.at[source],
            dst_ref=weighted.at[source],
            send_sem=weighted_send.at[dest],
            recv_sem=weighted_recv.at[source],
            device_id={"cells": dest},
            device_id_type=MESH,
        )

    def image_copy(dest, source):
        return pltpu.make_async_remote_copy(
            src_ref=image_out.at[dest],
            dst_ref=image_in.at[source],
            send_sem=image_send.at[dest],
            recv_sem=image_recv.at[source],
            device_id={"stations": dest},
            device_id_type=MESH,
        )

    def gs_copy(dest, source):
        return pltpu.make_async_remote_copy(
            src_ref=gram_s.at[source],
            dst_ref=gram_s.at[source],
            send_sem=gs_send.at[dest],
            recv_sem=gs_recv.at[source],
            device_id={"stations": dest},
            device_id_type=MESH,
        )

    def gc_copy(dest, source):
        return pltpu.make_async_remote_copy(
            src_ref=gram_c.at[source],
            dst_ref=gram_c.at[source],
            send_sem=gc_send.at[dest],
            recv_sem=gc_recv.at[source],
            device_id={"cells": dest},
            device_id_type=MESH,
        )

    cell_feat[...] = cell_features(plan_ref, depth_ref).astype(BF16)
    scale[...] = (depth_ref[...].astype(F32) + 1.0) * 2.0
    features = station_features(index_ref)
    padded = jnp.concatenate(
        [features, jnp.zeros((128 - FEATURES, stations), F32)], axis=0
    )
    station_feat[...] = padded.T[:, :FEATURES].astype(BF16)

    pl.semaphore_wait(barrier, n_cells - 1 + n_stations - 1)

    own_block = me_c // block_owners

    def forward_block(turn, carry):
        index = lax.rem(own_block + 1 + turn, blocks)
        start = pl.multiple_of(index * block, block)

        def column(step, running):
            left = pl.multiple_of(step * TILE, TILE)
            columns = pl.ds(left, TILE)
            factor2 = scale[:, columns]
            parts = []
            for piece in range(block // TILE):
                rows = pl.ds(start + piece * TILE, TILE)
                distance = matmul(station_feat[rows, :], cell_feat[:, columns])
                inverse = lax.rsqrt(distance)
                tile = (factor2 * inverse * inverse * inverse).astype(BF16)
                sens[rows, columns] = tile
                parts.append(running[piece] + matmul_nt(probes_ref[:, columns], tile))
            return tuple(parts)

        zero = jnp.zeros((k_rows, TILE), F32)
        totals = lax.fori_loop(
            0, cells // TILE, column, tuple(zero for _ in range(block // TILE))
        )
        station_scale = weight_ref[:, pl.ds(start, block)]
        field = jnp.concatenate(totals, axis=1) * (station_scale * station_scale)
        for part in range(block_owners):
            dest = index * block_owners + part
            field_out[dest] = field[:, part * own : (part + 1) * own]

            @pl.when(dest != me_c)
            def _():
                field_copy(dest).start()

        return carry

    lax.fori_loop(0, blocks, forward_block, 0)

    def add_field(step, running):
        source = peer_c(step)
        field_arrival(source).wait_recv()
        return running + field_in[source]

    total = lax.fori_loop(1, n_cells, add_field, field_out[me_c])
    weighted[me_c] = total.astype(BF16)

    def send_weighted(step, carry):
        weighted_copy(peer_c(step), me_c).start()
        return carry

    lax.fori_loop(1, n_cells, send_weighted, 0)

    def await_weighted(step, carry):
        weighted_copy(peer_c(step), peer_c(step)).wait_recv()
        return carry

    lax.fori_loop(1, n_cells, await_weighted, 0)

    offsets = [2, 1, 3, 0] if n_stations == 4 else list(range(n_stations - 1, -1, -1))
    image = None
    for offset in offsets:
        dest = peer_s(offset)
        columns = pl.ds(pl.multiple_of(dest * quarter, quarter), quarter)

        def backward(step, running):
            rows = pl.ds(pl.multiple_of(step * own, own), own)
            return running + matmul(weighted[step], sens[rows, columns])

        partial = lax.fori_loop(0, n_cells, backward, jnp.zeros((k_rows, quarter), F32))
        if offset:
            image_out[dest] = partial
            image_copy(dest, me_s).start()
        else:
            image = partial + reg_ref[:, columns] * probes_ref[:, columns].astype(F32)

    for step in range(1, n_stations):
        source = peer_s(step)
        image_copy(source, source).wait_recv()
        image = image + image_in[source]

    gram = matmul_nt(image, image, lax.Precision.HIGHEST)
    gram_s[me_s] = gram
    for step in range(1, n_stations):
        gs_copy(peer_s(step), me_s).start()
    for step in range(1, n_stations):
        gs_copy(peer_s(step), peer_s(step)).wait_recv()
    gram = gram_s[0]
    for source in range(1, n_stations):
        gram = gram + gram_s[source]
    gram_c[me_c] = gram

    def send_gram(step, carry):
        gc_copy(peer_c(step), me_c).start()
        return carry

    def await_gram(step, carry):
        gc_copy(peer_c(step), peer_c(step)).wait_recv()
        return carry

    lax.fori_loop(1, n_cells, send_gram, 0)
    lax.fori_loop(1, n_cells, await_gram, 0)
    gram = lax.fori_loop(1, n_cells, lambda s, r: r + gram_c[s], gram_c[0])

    row = lax.broadcasted_iota(jnp.int32, (k_rows, k_rows), 0)
    col = lax.broadcasted_iota(jnp.int32, (k_rows, k_rows), 1)
    left = gram / (cells * n_cells) + jnp.where(row == col, JITTER, 0.0)
    lower = jnp.zeros_like(left)
    row1 = row[:, 0:1]
    for j in range(k_rows):
        pivot = left[j : j + 1, j : j + 1]
        column = left[:, j : j + 1]
        lower = jnp.where((col == j) & (row >= j), column * lax.rsqrt(pivot), lower)
        ratio = jnp.where(row1 > j, column / pivot, 0.0)
        left = left - ratio * left[j : j + 1, :]
        image = image - ratio * image[j : j + 1, :]
    diagonal = jnp.sum(jnp.where(row == col, left, 0.0), axis=1, keepdims=True)
    basis_ref[...] = image * lax.rsqrt(diagonal)
    factor_ref[...] = lower

    def finish_c(step, carry):
        dest = peer_c(step)
        field_copy(dest).wait_send()
        weighted_copy(dest, me_c).wait_send()
        gc_copy(dest, me_c).wait_send()
        return carry

    lax.fori_loop(1, n_cells, finish_c, 0)
    for step in range(1, n_stations):
        dest = peer_s(step)
        image_copy(dest, me_s).wait_send()
        gs_copy(dest, me_s).wait_send()


def body(n_cells, n_stations, probes, reg_weight, cell_plan, cell_depth, station_index, station_weight):
    k_rows, cells = probes.shape
    stations = station_index.shape[1]
    own = stations // n_cells
    quarter = cells // n_stations
    dma = pltpu.SemaphoreType.DMA
    return pl.pallas_call(
        functools.partial(kernel, n_cells, n_stations),
        out_shape=(
            jax.ShapeDtypeStruct((k_rows, quarter), F32),
            jax.ShapeDtypeStruct((k_rows, k_rows), F32),
        ),
        in_specs=[pl.BlockSpec(memory_space=pltpu.VMEM)] * 6,
        out_specs=(pl.BlockSpec(memory_space=pltpu.VMEM),) * 2,
        scratch_shapes=[
            pltpu.VMEM((stations, cells), BF16),
            pltpu.VMEM((FEATURES, cells), BF16),
            pltpu.VMEM((stations, FEATURES), BF16),
            pltpu.VMEM((1, cells), F32),
            pltpu.VMEM((n_cells, k_rows, own), F32),
            pltpu.VMEM((n_cells, k_rows, own), F32),
            pltpu.VMEM((n_cells, k_rows, own), BF16),
            pltpu.VMEM((n_stations, k_rows, quarter), F32),
            pltpu.VMEM((n_stations, k_rows, quarter), F32),
            pltpu.VMEM((n_stations, k_rows, k_rows), F32),
            pltpu.VMEM((n_cells, k_rows, k_rows), F32),
            dma((n_cells,)),
            dma((n_cells,)),
            dma((n_cells,)),
            dma((n_cells,)),
            dma((n_stations,)),
            dma((n_stations,)),
            dma((n_stations,)),
            dma((n_stations,)),
            dma((n_cells,)),
            dma((n_cells,)),
        ],
        compiler_params=pltpu.CompilerParams(
            collective_id=0, has_side_effects=True, vmem_limit_bytes=56 * 1024 * 1024
        ),
    )(
        probes,
        reg_weight.reshape(1, -1),
        cell_plan,
        cell_depth.reshape(1, -1),
        station_index,
        station_weight.reshape(1, -1),
    )


def solution(mesh):
    return jax.shard_map(
        functools.partial(body, mesh.shape["cells"], mesh.shape["stations"]),
        mesh=mesh,
        in_specs=(
            P(None, "cells"),
            P("cells"),
            P(None, "cells"),
            P("cells"),
            P(None, "stations"),
            P("stations"),
        ),
        out_specs=(P(None, ("cells", "stations")), P()),
        check_vma=False,
    )
```

```python
import functools
import math

import jax
import jax.numpy as jnp
from jax import lax
from jax.experimental import pallas as pl
from jax.experimental.pallas import tpu as pltpu
from jax.sharding import PartitionSpec as P

JITTER = 1e-06
MESH = pl.DeviceIdType.MESH
F32 = jnp.float32
BF16 = jnp.bfloat16
TILE = 256
FEATURES = 16


def matmul(left, right):
    return jnp.dot(left, right, preferred_element_type=F32)


def matmul_nt(left, right, precision=None):
    return lax.dot_general(
        left, right, (((1,), (1,)), ((), ())), precision=precision, preferred_element_type=F32
    )


def cell_features(plan_ref, depth_ref):
    east = plan_ref[0:1, :] - 128
    north = plan_ref[1:2, :] - 128
    down = depth_ref[...] + 1
    square = east * east + north * north + down * down
    high = (square >> 8) << 8
    low = square & 255
    one = jnp.ones_like(square)
    zero = jnp.zeros_like(square)
    rows = [high, low, one, one, east, north, zero, zero]
    rows += [east, north, one, one, one, zero, zero, zero]
    return jnp.concatenate([row.astype(F32) for row in rows], axis=0)


def station_features(index_ref):
    east, north = index_ref[0:1, :], index_ref[1:2, :]
    whole_e, whole_n = (east >> 8) - 128, (north >> 8) - 128
    part_e, part_n = (east & 255) - 128, (north & 255) - 128
    square = whole_e * whole_e + whole_n * whole_n
    cross = 512 * (whole_e * part_e + whole_n * part_n) + part_e * part_e + part_n * part_n
    one = jnp.ones_like(square).astype(F32)
    zero = jnp.zeros_like(one)
    rows = [
        one,
        one,
        ((square >> 8) << 8).astype(F32),
        (square & 255).astype(F32),
        (-2 * whole_e).astype(F32),
        (-2 * whole_n).astype(F32),
        zero,
        zero,
        part_e.astype(F32) * (-2.0 / 256),
        part_n.astype(F32) * (-2.0 / 256),
        (cross >> 16).astype(F32),
        ((cross >> 8) & 255).astype(F32) * (1.0 / 256),
        (cross & 255).astype(F32) * (1.0 / 65536),
        zero,
        zero,
        zero,
    ]
    return jnp.concatenate(rows, axis=0)


def kernel(
    n_cells,
    n_stations,
    probes_ref,
    reg_ref,
    plan_ref,
    depth_ref,
    index_ref,
    weight_ref,
    basis_ref,
    factor_ref,
    sens,
    cell_feat,
    station_feat,
    scale,
    running,
    field_out,
    field_in,
    weighted,
    image_out,
    image_in,
    gram_s,
    gram_c,
    field_send,
    field_recv,
    weighted_send,
    weighted_recv,
    image_send,
    image_recv,
    gs_send,
    gs_recv,
    gc_send,
    gc_recv,
):
    k_rows, cells = probes_ref.shape
    stations = index_ref.shape[1]
    own = stations // n_cells
    quarter = cells // n_stations
    block = max(own, 512)
    block_owners = block // own
    blocks = stations // block
    me_c = lax.axis_index("cells")
    me_s = lax.axis_index("stations")

    def peer_c(step):
        return lax.rem(me_c + step, n_cells)

    def peer_s(step):
        return lax.rem(me_s + step, n_stations)

    barrier = pltpu.get_barrier_semaphore()

    def greet_c(step, carry):
        pl.semaphore_signal(barrier, inc=1, device_id={"cells": peer_c(step)}, device_id_type=MESH)
        return carry

    lax.fori_loop(1, n_cells, greet_c, 0)
    for step in range(1, n_stations):
        pl.semaphore_signal(
            barrier, inc=1, device_id={"stations": peer_s(step)}, device_id_type=MESH
        )

    def field_copy(dest):
        return pltpu.make_async_remote_copy(
            src_ref=field_out.at[dest],
            dst_ref=field_in.at[me_c],
            send_sem=field_send.at[dest],
            recv_sem=field_recv.at[me_c],
            device_id={"cells": dest},
            device_id_type=MESH,
        )

    def field_arrival(source):
        return pltpu.make_async_remote_copy(
            src_ref=field_out.at[source],
            dst_ref=field_in.at[source],
            send_sem=field_send.at[source],
            recv_sem=field_recv.at[source],
            device_id={"cells": source},
            device_id_type=MESH,
        )

    def weighted_copy(dest, source):
        return pltpu.make_async_remote_copy(
            src_ref=weighted.at[source],
            dst_ref=weighted.at[source],
            send_sem=weighted_send.at[dest],
            recv_sem=weighted_recv.at[source],
            device_id={"cells": dest},
            device_id_type=MESH,
        )

    def image_copy(dest, source):
        return pltpu.make_async_remote_copy(
            src_ref=image_out.at[dest],
            dst_ref=image_in.at[source],
            send_sem=image_send.at[dest],
            recv_sem=image_recv.at[source],
            device_id={"stations": dest},
            device_id_type=MESH,
        )

    def gs_copy(dest, source):
        return pltpu.make_async_remote_copy(
            src_ref=gram_s.at[source],
            dst_ref=gram_s.at[source],
            send_sem=gs_send.at[dest],
            recv_sem=gs_recv.at[source],
            device_id={"stations": dest},
            device_id_type=MESH,
        )

    def gc_copy(dest, source):
        return pltpu.make_async_remote_copy(
            src_ref=gram_c.at[source],
            dst_ref=gram_c.at[source],
            send_sem=gc_send.at[dest],
            recv_sem=gc_recv.at[source],
            device_id={"cells": dest},
            device_id_type=MESH,
        )

    cell_feat[...] = cell_features(plan_ref, depth_ref).astype(BF16)
    scale[...] = (depth_ref[...].astype(F32) + 1.0) * 2.0
    features = station_features(index_ref)
    padded = jnp.concatenate(
        [features, jnp.zeros((128 - FEATURES, stations), F32)], axis=0
    )
    station_feat[...] = padded.T[:, :FEATURES].astype(BF16)

    own_block = me_c // block_owners
    width = math.gcd(cells, 4 * TILE)
    chunks = cells // width
    pieces = block // TILE

    def place(turn):
        index = lax.rem(own_block + 1 + turn // chunks, blocks)
        return index, pl.multiple_of(index * block, block), lax.rem(turn, chunks)

    def make_tiles(turn):
        _, start, chunk = place(turn)
        for step in range(width // TILE):
            columns = pl.ds(pl.multiple_of(chunk * width + step * TILE, TILE), TILE)
            factor2 = scale[:, columns]
            for piece in range(pieces):
                rows = pl.ds(start + piece * TILE, TILE)
                distance = matmul(station_feat[rows, :], cell_feat[:, columns])
                inverse = lax.rsqrt(distance)
                sens[rows, columns] = (factor2 * inverse * inverse * inverse).astype(BF16)

    def use_tiles(turn):
        _, start, chunk = place(turn)
        columns = pl.ds(pl.multiple_of(chunk * width, width), width)
        vectors = probes_ref[:, columns]
        for piece in range(pieces):
            rows = pl.ds(start + piece * TILE, TILE)
            into = pl.ds(piece * TILE, TILE)
            before = jnp.where(chunk == 0, 0.0, running[:, into])
            running[:, into] = before + matmul_nt(vectors, sens[rows, columns])

    def send_field(turn):
        index, start, chunk = place(turn)

        @pl.when(chunk == chunks - 1)
        def _():
            station_scale = weight_ref[:, pl.ds(start, block)]
            field = running[...] * (station_scale * station_scale)
            for part in range(block_owners):
                dest = index * block_owners + part
                field_out[dest] = field[:, part * own : (part + 1) * own]

                @pl.when(dest != me_c)
                def _():
                    field_copy(dest).start()

    running[...] = jnp.zeros_like(running)
    make_tiles(0)
    pl.semaphore_wait(barrier, n_cells - 1 + n_stations - 1)

    def forward(turn, carry):
        use_tiles(turn - 1)
        make_tiles(turn)
        send_field(turn - 1)
        return carry

    lax.fori_loop(1, blocks * chunks, forward, 0)
    use_tiles(blocks * chunks - 1)
    send_field(blocks * chunks - 1)

    def add_field(step, before):
        source = peer_c(step)
        field_arrival(source).wait_recv()
        return before + field_in[source]

    total = lax.fori_loop(1, n_cells, add_field, field_out[me_c])
    weighted[me_c] = total.astype(BF16)

    def send_weighted(step, carry):
        weighted_copy(peer_c(step), me_c).start()
        return carry

    lax.fori_loop(1, n_cells, send_weighted, 0)

    def await_weighted(step, carry):
        weighted_copy(peer_c(step), peer_c(step)).wait_recv()
        return carry

    lax.fori_loop(1, n_cells, await_weighted, 0)

    offsets = [2, 1, 3, 0] if n_stations == 4 else list(range(n_stations - 1, -1, -1))
    image = None
    for offset in offsets:
        dest = peer_s(offset)
        columns = pl.ds(pl.multiple_of(dest * quarter, quarter), quarter)

        def backward(step, before):
            rows = pl.ds(pl.multiple_of(step * own, own), own)
            return before + matmul(weighted[step], sens[rows, columns])

        partial = lax.fori_loop(0, n_cells, backward, jnp.zeros((k_rows, quarter), F32), unroll=2)
        if offset:
            image_out[dest] = partial
            image_copy(dest, me_s).start()
        else:
            image = partial + reg_ref[:, columns] * probes_ref[:, columns].astype(F32)

    for step in range(1, n_stations):
        source = peer_s(step)
        image_copy(source, source).wait_recv()
        image = image + image_in[source]

    gram = matmul_nt(image, image, lax.Precision.HIGHEST)
    gram_s[me_s] = gram
    for step in range(1, n_stations):
        gs_copy(peer_s(step), me_s).start()
    for step in range(1, n_stations):
        gs_copy(peer_s(step), peer_s(step)).wait_recv()
    gram = gram_s[0]
    for source in range(1, n_stations):
        gram = gram + gram_s[source]
    gram_c[me_c] = gram

    def send_gram(step, carry):
        gc_copy(peer_c(step), me_c).start()
        return carry

    def await_gram(step, carry):
        gc_copy(peer_c(step), peer_c(step)).wait_recv()
        return carry

    lax.fori_loop(1, n_cells, send_gram, 0)
    lax.fori_loop(1, n_cells, await_gram, 0)
    gram = lax.fori_loop(1, n_cells, lambda s, r: r + gram_c[s], gram_c[0])

    row = lax.broadcasted_iota(jnp.int32, (k_rows, k_rows), 0)
    col = lax.broadcasted_iota(jnp.int32, (k_rows, k_rows), 1)
    left = gram / (cells * n_cells) + jnp.where(row == col, JITTER, 0.0)
    lower = jnp.zeros_like(left)
    row1 = row[:, 0:1]
    for j in range(k_rows):
        pivot = left[j : j + 1, j : j + 1]
        column = left[:, j : j + 1]
        lower = jnp.where((col == j) & (row >= j), column * lax.rsqrt(pivot), lower)
        ratio = jnp.where(row1 > j, column / pivot, 0.0)
        left = left - ratio * left[j : j + 1, :]
        image = image - ratio * image[j : j + 1, :]
    diagonal = jnp.sum(jnp.where(row == col, left, 0.0), axis=1, keepdims=True)
    basis_ref[...] = image * lax.rsqrt(diagonal)
    factor_ref[...] = lower

    def finish_c(step, carry):
        dest = peer_c(step)
        field_copy(dest).wait_send()
        weighted_copy(dest, me_c).wait_send()
        gc_copy(dest, me_c).wait_send()
        return carry

    lax.fori_loop(1, n_cells, finish_c, 0)
    for step in range(1, n_stations):
        dest = peer_s(step)
        image_copy(dest, me_s).wait_send()
        gs_copy(dest, me_s).wait_send()


def body(n_cells, n_stations, probes, reg_weight, cell_plan, cell_depth, station_index, station_weight):
    k_rows, cells = probes.shape
    stations = station_index.shape[1]
    own = stations // n_cells
    quarter = cells // n_stations
    dma = pltpu.SemaphoreType.DMA
    return pl.pallas_call(
        functools.partial(kernel, n_cells, n_stations),
        out_shape=(
            jax.ShapeDtypeStruct((k_rows, quarter), F32),
            jax.ShapeDtypeStruct((k_rows, k_rows), F32),
        ),
        in_specs=[pl.BlockSpec(memory_space=pltpu.VMEM)] * 6,
        out_specs=(pl.BlockSpec(memory_space=pltpu.VMEM),) * 2,
        scratch_shapes=[
            pltpu.VMEM((stations, cells), BF16),
            pltpu.VMEM((FEATURES, cells), BF16),
            pltpu.VMEM((stations, FEATURES), BF16),
            pltpu.VMEM((1, cells), F32),
            pltpu.VMEM((k_rows, max(own, 512)), F32),
            pltpu.VMEM((n_cells, k_rows, own), F32),
            pltpu.VMEM((n_cells, k_rows, own), F32),
            pltpu.VMEM((n_cells, k_rows, own), BF16),
            pltpu.VMEM((n_stations, k_rows, quarter), F32),
            pltpu.VMEM((n_stations, k_rows, quarter), F32),
            pltpu.VMEM((n_stations, k_rows, k_rows), F32),
            pltpu.VMEM((n_cells, k_rows, k_rows), F32),
            dma((n_cells,)),
            dma((n_cells,)),
            dma((n_cells,)),
            dma((n_cells,)),
            dma((n_stations,)),
            dma((n_stations,)),
            dma((n_stations,)),
            dma((n_stations,)),
            dma((n_cells,)),
            dma((n_cells,)),
        ],
        compiler_params=pltpu.CompilerParams(
            collective_id=0, has_side_effects=True, vmem_limit_bytes=56 * 1024 * 1024
        ),
    )(
        probes,
        reg_weight.reshape(1, -1),
        cell_plan,
        cell_depth.reshape(1, -1),
        station_index,
        station_weight.reshape(1, -1),
    )


def solution(mesh):
    return jax.shard_map(
        functools.partial(body, mesh.shape["cells"], mesh.shape["stations"]),
        mesh=mesh,
        in_specs=(
            P(None, "cells"),
            P("cells"),
            P(None, "cells"),
            P("cells"),
            P(None, "stations"),
            P("stations"),
        ),
        out_specs=(P(None, ("cells", "stations")), P()),
        check_vma=False,
    )
```

```python
import functools
import math

import jax
import jax.numpy as jnp
from jax import lax
from jax.experimental import pallas as pl
from jax.experimental.pallas import tpu as pltpu
from jax.sharding import PartitionSpec as P

JITTER = 1e-06
MESH = pl.DeviceIdType.MESH
F32 = jnp.float32
BF16 = jnp.bfloat16
TILE = 256
FEATURES = 16


def matmul(left, right):
    return jnp.dot(left, right, preferred_element_type=F32)


def matmul_nt(left, right, precision=None):
    return lax.dot_general(
        left, right, (((1,), (1,)), ((), ())), precision=precision, preferred_element_type=F32
    )


def cell_features(plan_ref, depth_ref):
    east = plan_ref[0:1, :] - 128
    north = plan_ref[1:2, :] - 128
    down = depth_ref[...] + 1
    square = east * east + north * north + down * down
    high = (square >> 8) << 8
    low = square & 255
    one = jnp.ones_like(square)
    zero = jnp.zeros_like(square)
    rows = [high, low, one, one, east, north, zero, zero]
    rows += [east, north, one, one, one, zero, zero, zero]
    return jnp.concatenate([row.astype(F32) for row in rows], axis=0)


def station_features(index_ref):
    east, north = index_ref[0:1, :], index_ref[1:2, :]
    whole_e, whole_n = (east >> 8) - 128, (north >> 8) - 128
    part_e, part_n = (east & 255) - 128, (north & 255) - 128
    square = whole_e * whole_e + whole_n * whole_n
    cross = 512 * (whole_e * part_e + whole_n * part_n) + part_e * part_e + part_n * part_n
    one = jnp.ones_like(square).astype(F32)
    zero = jnp.zeros_like(one)
    rows = [
        one,
        one,
        ((square >> 8) << 8).astype(F32),
        (square & 255).astype(F32),
        (-2 * whole_e).astype(F32),
        (-2 * whole_n).astype(F32),
        zero,
        zero,
        part_e.astype(F32) * (-2.0 / 256),
        part_n.astype(F32) * (-2.0 / 256),
        (cross >> 16).astype(F32),
        ((cross >> 8) & 255).astype(F32) * (1.0 / 256),
        (cross & 255).astype(F32) * (1.0 / 65536),
        zero,
        zero,
        zero,
    ]
    return jnp.concatenate(rows, axis=0)


def kernel(
    n_cells,
    n_stations,
    probes_ref,
    reg_ref,
    plan_ref,
    depth_ref,
    index_ref,
    weight_ref,
    basis_ref,
    factor_ref,
    sens,
    cell_feat,
    station_feat,
    scale,
    running,
    field_out,
    field_in,
    weighted,
    image_out,
    image_in,
    gram_s,
    gram_c,
    field_send,
    field_recv,
    weighted_send,
    weighted_recv,
    image_send,
    image_recv,
    gs_send,
    gs_recv,
    gc_send,
    gc_recv,
):
    k_rows, cells = probes_ref.shape
    stations = index_ref.shape[1]
    own = stations // n_cells
    quarter = cells // n_stations
    block = max(own, 512)
    block_owners = block // own
    blocks = stations // block
    me_c = lax.axis_index("cells")
    me_s = lax.axis_index("stations")

    def peer_c(step):
        return lax.rem(me_c + step, n_cells)

    def peer_s(step):
        return lax.rem(me_s + step, n_stations)

    barrier = pltpu.get_barrier_semaphore()

    def greet_c(step, carry):
        pl.semaphore_signal(barrier, inc=1, device_id={"cells": peer_c(step)}, device_id_type=MESH)
        return carry

    lax.fori_loop(1, n_cells, greet_c, 0)
    for step in range(1, n_stations):
        pl.semaphore_signal(
            barrier, inc=1, device_id={"stations": peer_s(step)}, device_id_type=MESH
        )

    def field_copy(dest):
        return pltpu.make_async_remote_copy(
            src_ref=field_out.at[dest],
            dst_ref=field_in.at[me_c],
            send_sem=field_send.at[dest],
            recv_sem=field_recv.at[me_c],
            device_id={"cells": dest},
            device_id_type=MESH,
        )

    def field_arrival(source):
        return pltpu.make_async_remote_copy(
            src_ref=field_out.at[source],
            dst_ref=field_in.at[source],
            send_sem=field_send.at[source],
            recv_sem=field_recv.at[source],
            device_id={"cells": source},
            device_id_type=MESH,
        )

    def weighted_copy(dest, source):
        return pltpu.make_async_remote_copy(
            src_ref=weighted.at[source],
            dst_ref=weighted.at[source],
            send_sem=weighted_send.at[dest],
            recv_sem=weighted_recv.at[source],
            device_id={"cells": dest},
            device_id_type=MESH,
        )

    def image_copy(dest, source):
        return pltpu.make_async_remote_copy(
            src_ref=image_out.at[dest],
            dst_ref=image_in.at[source],
            send_sem=image_send.at[dest],
            recv_sem=image_recv.at[source],
            device_id={"stations": dest},
            device_id_type=MESH,
        )

    def gs_copy(dest, source):
        return pltpu.make_async_remote_copy(
            src_ref=gram_s.at[source],
            dst_ref=gram_s.at[source],
            send_sem=gs_send.at[dest],
            recv_sem=gs_recv.at[source],
            device_id={"stations": dest},
            device_id_type=MESH,
        )

    def gc_copy(dest, source):
        return pltpu.make_async_remote_copy(
            src_ref=gram_c.at[source],
            dst_ref=gram_c.at[source],
            send_sem=gc_send.at[dest],
            recv_sem=gc_recv.at[source],
            device_id={"cells": dest},
            device_id_type=MESH,
        )

    cell_feat[...] = cell_features(plan_ref, depth_ref).astype(BF16)
    scale[...] = (depth_ref[...].astype(F32) + 1.0) * 2.0
    features = station_features(index_ref)
    padded = jnp.concatenate(
        [features, jnp.zeros((128 - FEATURES, stations), F32)], axis=0
    )
    station_feat[...] = padded.T[:, :FEATURES].astype(BF16)

    own_block = me_c // block_owners
    width = math.gcd(cells, 4 * TILE)
    chunks = cells // width
    pieces = block // TILE

    def place(turn):
        index = turn // chunks
        return index, pl.multiple_of(index * block, block), lax.rem(turn, chunks)

    def make_tiles(turn):
        _, start, chunk = place(turn)
        for step in range(width // TILE):
            columns = pl.ds(pl.multiple_of(chunk * width + step * TILE, TILE), TILE)
            factor2 = scale[:, columns]
            for piece in range(pieces):
                rows = pl.ds(start + piece * TILE, TILE)
                distance = matmul(station_feat[rows, :], cell_feat[:, columns])
                inverse = lax.rsqrt(distance)
                sens[rows, columns] = (factor2 * inverse * inverse * inverse).astype(BF16)

    def use_tiles(turn):
        _, start, chunk = place(turn)
        columns = pl.ds(pl.multiple_of(chunk * width, width), width)
        vectors = probes_ref[:, columns]
        for piece in range(pieces):
            rows = pl.ds(start + piece * TILE, TILE)
            into = pl.ds(piece * TILE, TILE)
            before = jnp.where(chunk == 0, 0.0, running[:, into])
            running[:, into] = before + matmul_nt(vectors, sens[rows, columns])

    def send_field(turn):
        index, start, chunk = place(turn)

        @pl.when(chunk == chunks - 1)
        def _():
            station_scale = weight_ref[:, pl.ds(start, block)]
            field = running[...] * (station_scale * station_scale)
            for part in range(block_owners):
                dest = index * block_owners + part
                field_out[dest] = field[:, part * own : (part + 1) * own]

                @pl.when(dest != me_c)
                def _():
                    field_copy(dest).start()

    def collect_field():
        def add_field(step, before):
            source = peer_c(step)
            field_arrival(source).wait_recv()
            return before + field_in[source]

        total = lax.fori_loop(1, n_cells, add_field, field_out[me_c])
        weighted[me_c] = total.astype(BF16)

        def send_weighted(step, carry):
            weighted_copy(peer_c(step), me_c).start()
            return carry

        lax.fori_loop(1, n_cells, send_weighted, 0)

    running[...] = jnp.zeros_like(running)
    make_tiles(0)
    pl.semaphore_wait(barrier, n_cells - 1 + n_stations - 1)

    def forward(turn, carry):
        use_tiles(turn - 1)
        make_tiles(turn)
        send_field(turn - 1)

        @pl.when(turn - 1 == (own_block + 2) * chunks - 2)
        def _():
            collect_field()

        return carry

    lax.fori_loop(1, blocks * chunks, forward, 0)
    use_tiles(blocks * chunks - 1)
    send_field(blocks * chunks - 1)

    early = n_cells - min(2, blocks) * block_owners
    image_out[...] = jnp.zeros_like(image_out)

    def await_weighted(source):
        @pl.when(source != me_c)
        def _():
            weighted_copy(source, source).wait_recv()

    def backward_early(source, carry):
        @pl.when((source == early // 3) & (own_block == blocks - 1))
        def _():
            collect_field()

        await_weighted(source)
        rows = pl.ds(pl.multiple_of(source * own, own), own)
        for part in range(n_stations):
            columns = pl.ds(part * quarter, quarter)
            image_out[part] += matmul(weighted[source], sens[rows, columns])
        return carry

    lax.fori_loop(0, early, backward_early, 0)

    def await_late(source, carry):
        await_weighted(source)
        return carry

    lax.fori_loop(early, n_cells, await_late, 0)

    offsets = [2, 1, 3, 0] if n_stations == 4 else list(range(n_stations - 1, -1, -1))
    image = None
    for offset in offsets:
        dest = peer_s(offset)
        columns = pl.ds(pl.multiple_of(dest * quarter, quarter), quarter)

        def backward(source, before):
            rows = pl.ds(pl.multiple_of(source * own, own), own)
            return before + matmul(weighted[source], sens[rows, columns])

        partial = lax.fori_loop(early, n_cells, backward, image_out[dest], unroll=2)
        if offset:
            image_out[dest] = partial
            image_copy(dest, me_s).start()
        else:
            image = partial + reg_ref[:, columns] * probes_ref[:, columns].astype(F32)

    for step in range(1, n_stations):
        source = peer_s(step)
        image_copy(source, source).wait_recv()
        image = image + image_in[source]

    gram = matmul_nt(image, image, lax.Precision.HIGHEST)
    gram_s[me_s] = gram
    for step in range(1, n_stations):
        gs_copy(peer_s(step), me_s).start()
    for step in range(1, n_stations):
        gs_copy(peer_s(step), peer_s(step)).wait_recv()
    gram = gram_s[0]
    for source in range(1, n_stations):
        gram = gram + gram_s[source]
    gram_c[me_c] = gram

    def send_gram(step, carry):
        gc_copy(peer_c(step), me_c).start()
        return carry

    def await_gram(step, carry):
        gc_copy(peer_c(step), peer_c(step)).wait_recv()
        return carry

    lax.fori_loop(1, n_cells, send_gram, 0)
    lax.fori_loop(1, n_cells, await_gram, 0)
    gram = lax.fori_loop(1, n_cells, lambda s, r: r + gram_c[s], gram_c[0])

    row = lax.broadcasted_iota(jnp.int32, (k_rows, k_rows), 0)
    col = lax.broadcasted_iota(jnp.int32, (k_rows, k_rows), 1)
    left = gram / (cells * n_cells) + jnp.where(row == col, JITTER, 0.0)
    lower = jnp.zeros_like(left)
    row1 = row[:, 0:1]
    for j in range(k_rows):
        pivot = left[j : j + 1, j : j + 1]
        column = left[:, j : j + 1]
        lower = jnp.where((col == j) & (row >= j), column * lax.rsqrt(pivot), lower)
        ratio = jnp.where(row1 > j, column / pivot, 0.0)
        left = left - ratio * left[j : j + 1, :]
        image = image - ratio * image[j : j + 1, :]
    diagonal = jnp.sum(jnp.where(row == col, left, 0.0), axis=1, keepdims=True)
    basis_ref[...] = image * lax.rsqrt(diagonal)
    factor_ref[...] = lower

    def finish_c(step, carry):
        dest = peer_c(step)
        field_copy(dest).wait_send()
        weighted_copy(dest, me_c).wait_send()
        gc_copy(dest, me_c).wait_send()
        return carry

    lax.fori_loop(1, n_cells, finish_c, 0)
    for step in range(1, n_stations):
        dest = peer_s(step)
        image_copy(dest, me_s).wait_send()
        gs_copy(dest, me_s).wait_send()


def body(n_cells, n_stations, probes, reg_weight, cell_plan, cell_depth, station_index, station_weight):
    k_rows, cells = probes.shape
    stations = station_index.shape[1]
    own = stations // n_cells
    quarter = cells // n_stations
    dma = pltpu.SemaphoreType.DMA
    return pl.pallas_call(
        functools.partial(kernel, n_cells, n_stations),
        out_shape=(
            jax.ShapeDtypeStruct((k_rows, quarter), F32),
            jax.ShapeDtypeStruct((k_rows, k_rows), F32),
        ),
        in_specs=[pl.BlockSpec(memory_space=pltpu.VMEM)] * 6,
        out_specs=(pl.BlockSpec(memory_space=pltpu.VMEM),) * 2,
        scratch_shapes=[
            pltpu.VMEM((stations, cells), BF16),
            pltpu.VMEM((FEATURES, cells), BF16),
            pltpu.VMEM((stations, FEATURES), BF16),
            pltpu.VMEM((1, cells), F32),
            pltpu.VMEM((k_rows, max(own, 512)), F32),
            pltpu.VMEM((n_cells, k_rows, own), F32),
            pltpu.VMEM((n_cells, k_rows, own), F32),
            pltpu.VMEM((n_cells, k_rows, own), BF16),
            pltpu.VMEM((n_stations, k_rows, quarter), F32),
            pltpu.VMEM((n_stations, k_rows, quarter), F32),
            pltpu.VMEM((n_stations, k_rows, k_rows), F32),
            pltpu.VMEM((n_cells, k_rows, k_rows), F32),
            dma((n_cells,)),
            dma((n_cells,)),
            dma((n_cells,)),
            dma((n_cells,)),
            dma((n_stations,)),
            dma((n_stations,)),
            dma((n_stations,)),
            dma((n_stations,)),
            dma((n_cells,)),
            dma((n_cells,)),
        ],
        compiler_params=pltpu.CompilerParams(
            collective_id=0, has_side_effects=True, vmem_limit_bytes=56 * 1024 * 1024
        ),
    )(
        probes,
        reg_weight.reshape(1, -1),
        cell_plan,
        cell_depth.reshape(1, -1),
        station_index,
        station_weight.reshape(1, -1),
    )


def solution(mesh):
    return jax.shard_map(
        functools.partial(body, mesh.shape["cells"], mesh.shape["stations"]),
        mesh=mesh,
        in_specs=(
            P(None, "cells"),
            P("cells"),
            P(None, "cells"),
            P("cells"),
            P(None, "stations"),
            P("stations"),
        ),
        out_specs=(P(None, ("cells", "stations")), P()),
        check_vma=False,
    )
```

```python
import functools
import math

import jax
import jax.numpy as jnp
from jax import lax
from jax.experimental import pallas as pl
from jax.experimental.pallas import tpu as pltpu
from jax.sharding import PartitionSpec as P

JITTER = 1e-06
MESH = pl.DeviceIdType.MESH
F32 = jnp.float32
BF16 = jnp.bfloat16
TILE = 256
FEATURES = 16


def matmul(left, right):
    return jnp.dot(left, right, preferred_element_type=F32)


def matmul_nt(left, right, precision=None):
    return lax.dot_general(
        left, right, (((1,), (1,)), ((), ())), precision=precision, preferred_element_type=F32
    )


def cell_features(plan_ref, depth_ref):
    east = plan_ref[0:1, :] - 128
    north = plan_ref[1:2, :] - 128
    down = depth_ref[...] + 1
    square = east * east + north * north + down * down
    high = (square >> 8) << 8
    low = square & 255
    one = jnp.ones_like(square)
    zero = jnp.zeros_like(square)
    rows = [high, low, one, one, east, north, zero, zero]
    rows += [east, north, one, one, one, zero, zero, zero]
    return jnp.concatenate([row.astype(F32) for row in rows], axis=0)


def station_features(index_ref):
    east, north = index_ref[0:1, :], index_ref[1:2, :]
    whole_e, whole_n = (east >> 8) - 128, (north >> 8) - 128
    part_e, part_n = (east & 255) - 128, (north & 255) - 128
    square = whole_e * whole_e + whole_n * whole_n
    cross = 512 * (whole_e * part_e + whole_n * part_n) + part_e * part_e + part_n * part_n
    one = jnp.ones_like(square).astype(F32)
    zero = jnp.zeros_like(one)
    rows = [
        one,
        one,
        ((square >> 8) << 8).astype(F32),
        (square & 255).astype(F32),
        (-2 * whole_e).astype(F32),
        (-2 * whole_n).astype(F32),
        zero,
        zero,
        part_e.astype(F32) * (-2.0 / 256),
        part_n.astype(F32) * (-2.0 / 256),
        (cross >> 16).astype(F32),
        ((cross >> 8) & 255).astype(F32) * (1.0 / 256),
        (cross & 255).astype(F32) * (1.0 / 65536),
        zero,
        zero,
        zero,
    ]
    return jnp.concatenate(rows, axis=0)


def kernel(
    n_cells,
    n_stations,
    probes_ref,
    reg_ref,
    plan_ref,
    depth_ref,
    index_ref,
    weight_ref,
    basis_ref,
    factor_ref,
    sens,
    cell_feat,
    station_feat,
    scale,
    running,
    field_out,
    field_in,
    weighted,
    image_out,
    image_in,
    gram_s,
    gram_c,
    field_send,
    field_recv,
    weighted_send,
    weighted_recv,
    image_send,
    image_recv,
    gs_send,
    gs_recv,
    gc_send,
    gc_recv,
):
    k_rows, cells = probes_ref.shape
    stations = index_ref.shape[1]
    own = stations // n_cells
    quarter = cells // n_stations
    block = max(own, 512)
    block_owners = block // own
    blocks = stations // block
    me_c = lax.axis_index("cells")
    me_s = lax.axis_index("stations")

    def peer_c(step):
        return lax.rem(me_c + step, n_cells)

    def peer_s(step):
        return lax.rem(me_s + step, n_stations)

    barrier = pltpu.get_barrier_semaphore()

    def greet_c(step, carry):
        pl.semaphore_signal(barrier, inc=1, device_id={"cells": peer_c(step)}, device_id_type=MESH)
        return carry

    lax.fori_loop(1, n_cells, greet_c, 0)
    for step in range(1, n_stations):
        pl.semaphore_signal(
            barrier, inc=1, device_id={"stations": peer_s(step)}, device_id_type=MESH
        )

    def field_copy(dest):
        return pltpu.make_async_remote_copy(
            src_ref=field_out.at[dest],
            dst_ref=field_in.at[me_c],
            send_sem=field_send.at[dest],
            recv_sem=field_recv.at[me_c],
            device_id={"cells": dest},
            device_id_type=MESH,
        )

    def field_arrival(source):
        return pltpu.make_async_remote_copy(
            src_ref=field_out.at[source],
            dst_ref=field_in.at[source],
            send_sem=field_send.at[source],
            recv_sem=field_recv.at[source],
            device_id={"cells": source},
            device_id_type=MESH,
        )

    def weighted_copy(dest, source):
        return pltpu.make_async_remote_copy(
            src_ref=weighted.at[source],
            dst_ref=weighted.at[source],
            send_sem=weighted_send.at[dest],
            recv_sem=weighted_recv.at[source],
            device_id={"cells": dest},
            device_id_type=MESH,
        )

    def image_copy(dest, source):
        return pltpu.make_async_remote_copy(
            src_ref=image_out.at[dest],
            dst_ref=image_in.at[source],
            send_sem=image_send.at[dest],
            recv_sem=image_recv.at[source],
            device_id={"stations": dest},
            device_id_type=MESH,
        )

    def gs_copy(dest, source):
        return pltpu.make_async_remote_copy(
            src_ref=gram_s.at[source],
            dst_ref=gram_s.at[source],
            send_sem=gs_send.at[dest],
            recv_sem=gs_recv.at[source],
            device_id={"stations": dest},
            device_id_type=MESH,
        )

    def gc_copy(dest, source):
        return pltpu.make_async_remote_copy(
            src_ref=gram_c.at[source],
            dst_ref=gram_c.at[source],
            send_sem=gc_send.at[dest],
            recv_sem=gc_recv.at[source],
            device_id={"cells": dest},
            device_id_type=MESH,
        )

    cell_feat[...] = cell_features(plan_ref, depth_ref).astype(BF16)
    scale[...] = (depth_ref[...].astype(F32) + 1.0) * 2.0
    features = station_features(index_ref)
    padded = jnp.concatenate(
        [features, jnp.zeros((128 - FEATURES, stations), F32)], axis=0
    )
    station_feat[...] = padded.T[:, :FEATURES].astype(BF16)

    own_block = me_c // block_owners
    width = math.gcd(cells, 8 * TILE)
    chunks = cells // width
    pieces = block // TILE

    def place(turn):
        index = lax.rem(own_block + 1 + turn // chunks, blocks)
        return index, pl.multiple_of(index * block, block), lax.rem(turn, chunks)

    def make_tiles(turn):
        _, start, chunk = place(turn)
        for step in range(width // TILE):
            columns = pl.ds(pl.multiple_of(chunk * width + step * TILE, TILE), TILE)
            factor2 = scale[:, columns]
            rows = pl.ds(start, block)
            distance = matmul(station_feat[rows, :], cell_feat[:, columns])
            inverse = lax.rsqrt(distance)
            sens[rows, columns] = (factor2 * inverse * inverse * inverse).astype(BF16)

    def use_tiles(turn):
        _, start, chunk = place(turn)
        columns = pl.ds(pl.multiple_of(chunk * width, width), width)
        vectors = probes_ref[:, columns]
        for piece in range(pieces):
            rows = pl.ds(start + piece * TILE, TILE)
            into = pl.ds(piece * TILE, TILE)
            before = jnp.where(chunk == 0, 0.0, running[:, into])
            running[:, into] = before + matmul_nt(vectors, sens[rows, columns])

    def send_field(turn):
        index, start, chunk = place(turn)

        @pl.when(chunk == chunks - 1)
        def _():
            station_scale = weight_ref[:, pl.ds(start, block)]
            field = running[...] * (station_scale * station_scale)
            for part in range(block_owners):
                dest = index * block_owners + part
                field_out[dest] = field[:, part * own : (part + 1) * own]

                @pl.when(dest != me_c)
                def _():
                    field_copy(dest).start()

    running[...] = jnp.zeros_like(running)
    make_tiles(0)
    pl.semaphore_wait(barrier, n_cells - 1 + n_stations - 1)

    def forward(turn, carry):
        use_tiles(turn - 1)
        make_tiles(turn)
        send_field(turn - 1)
        return carry

    lax.fori_loop(1, blocks * chunks, forward, 0)
    use_tiles(blocks * chunks - 1)
    send_field(blocks * chunks - 1)

    def add_field(step, before):
        source = peer_c(step)
        field_arrival(source).wait_recv()
        return before + field_in[source]

    total = lax.fori_loop(1, n_cells, add_field, field_out[me_c])
    weighted[me_c] = total.astype(BF16)

    def send_weighted(step, carry):
        weighted_copy(peer_c(step), me_c).start()
        return carry

    lax.fori_loop(1, n_cells, send_weighted, 0)

    def await_weighted(step, carry):
        weighted_copy(peer_c(step), peer_c(step)).wait_recv()
        return carry

    lax.fori_loop(1, n_cells, await_weighted, 0)

    offsets = [2, 1, 3, 0] if n_stations == 4 else list(range(n_stations - 1, -1, -1))
    image = None
    for offset in offsets:
        dest = peer_s(offset)
        columns = pl.ds(pl.multiple_of(dest * quarter, quarter), quarter)

        def backward(step, before):
            rows = pl.ds(pl.multiple_of(step * own, own), own)
            return before + matmul(weighted[step], sens[rows, columns])

        partial = lax.fori_loop(0, n_cells, backward, jnp.zeros((k_rows, quarter), F32), unroll=4)
        if offset:
            image_out[dest] = partial
            image_copy(dest, me_s).start()
        else:
            image = partial + reg_ref[:, columns] * probes_ref[:, columns].astype(F32)

    for step in range(1, n_stations):
        source = peer_s(step)
        image_copy(source, source).wait_recv()
        image = image + image_in[source]

    gram = matmul_nt(image, image, lax.Precision.HIGHEST)
    gram_s[me_s] = gram
    for step in range(1, n_stations):
        gs_copy(peer_s(step), me_s).start()
    for step in range(1, n_stations):
        gs_copy(peer_s(step), peer_s(step)).wait_recv()
    gram = gram_s[0]
    for source in range(1, n_stations):
        gram = gram + gram_s[source]
    gram_c[me_c] = gram

    def send_gram(step, carry):
        gc_copy(peer_c(step), me_c).start()
        return carry

    def await_gram(step, carry):
        gc_copy(peer_c(step), peer_c(step)).wait_recv()
        return carry

    lax.fori_loop(1, n_cells, send_gram, 0)
    lax.fori_loop(1, n_cells, await_gram, 0)
    gram = lax.fori_loop(1, n_cells, lambda s, r: r + gram_c[s], gram_c[0])

    row = lax.broadcasted_iota(jnp.int32, (k_rows, k_rows), 0)
    col = lax.broadcasted_iota(jnp.int32, (k_rows, k_rows), 1)
    left = gram / (cells * n_cells) + jnp.where(row == col, JITTER, 0.0)
    lower = jnp.zeros_like(left)
    row1 = row[:, 0:1]
    for j in range(k_rows):
        pivot = left[j : j + 1, j : j + 1]
        column = left[:, j : j + 1]
        lower = jnp.where((col == j) & (row >= j), column * lax.rsqrt(pivot), lower)
        ratio = jnp.where(row1 > j, column / pivot, 0.0)
        left = left - ratio * left[j : j + 1, :]
        image = image - ratio * image[j : j + 1, :]
    diagonal = jnp.sum(jnp.where(row == col, left, 0.0), axis=1, keepdims=True)
    basis_ref[...] = image * lax.rsqrt(diagonal)
    factor_ref[...] = lower

    def finish_c(step, carry):
        dest = peer_c(step)
        field_copy(dest).wait_send()
        weighted_copy(dest, me_c).wait_send()
        gc_copy(dest, me_c).wait_send()
        return carry

    lax.fori_loop(1, n_cells, finish_c, 0)
    for step in range(1, n_stations):
        dest = peer_s(step)
        image_copy(dest, me_s).wait_send()
        gs_copy(dest, me_s).wait_send()


def body(n_cells, n_stations, probes, reg_weight, cell_plan, cell_depth, station_index, station_weight):
    k_rows, cells = probes.shape
    stations = station_index.shape[1]
    own = stations // n_cells
    quarter = cells // n_stations
    dma = pltpu.SemaphoreType.DMA
    return pl.pallas_call(
        functools.partial(kernel, n_cells, n_stations),
        out_shape=(
            jax.ShapeDtypeStruct((k_rows, quarter), F32),
            jax.ShapeDtypeStruct((k_rows, k_rows), F32),
        ),
        in_specs=[pl.BlockSpec(memory_space=pltpu.VMEM)] * 6,
        out_specs=(pl.BlockSpec(memory_space=pltpu.VMEM),) * 2,
        scratch_shapes=[
            pltpu.VMEM((stations, cells), BF16),
            pltpu.VMEM((FEATURES, cells), BF16),
            pltpu.VMEM((stations, FEATURES), BF16),
            pltpu.VMEM((1, cells), F32),
            pltpu.VMEM((k_rows, max(own, 512)), F32),
            pltpu.VMEM((n_cells, k_rows, own), F32),
            pltpu.VMEM((n_cells, k_rows, own), F32),
            pltpu.VMEM((n_cells, k_rows, own), BF16),
            pltpu.VMEM((n_stations, k_rows, quarter), F32),
            pltpu.VMEM((n_stations, k_rows, quarter), F32),
            pltpu.VMEM((n_stations, k_rows, k_rows), F32),
            pltpu.VMEM((n_cells, k_rows, k_rows), F32),
            dma((n_cells,)),
            dma((n_cells,)),
            dma((n_cells,)),
            dma((n_cells,)),
            dma((n_stations,)),
            dma((n_stations,)),
            dma((n_stations,)),
            dma((n_stations,)),
            dma((n_cells,)),
            dma((n_cells,)),
        ],
        compiler_params=pltpu.CompilerParams(
            collective_id=0, has_side_effects=True, vmem_limit_bytes=56 * 1024 * 1024
        ),
    )(
        probes,
        reg_weight.reshape(1, -1),
        cell_plan,
        cell_depth.reshape(1, -1),
        station_index,
        station_weight.reshape(1, -1),
    )


def solution(mesh):
    return jax.shard_map(
        functools.partial(body, mesh.shape["cells"], mesh.shape["stations"]),
        mesh=mesh,
        in_specs=(
            P(None, "cells"),
            P("cells"),
            P(None, "cells"),
            P("cells"),
            P(None, "stations"),
            P("stations"),
        ),
        out_specs=(P(None, ("cells", "stations")), P()),
        check_vma=False,
    )
```

```python
import functools
import math

import jax
import jax.numpy as jnp
from jax import lax
from jax.experimental import pallas as pl
from jax.experimental.pallas import tpu as pltpu
from jax.sharding import PartitionSpec as P

JITTER = 1e-06
MESH = pl.DeviceIdType.MESH
F32 = jnp.float32
BF16 = jnp.bfloat16
TILE = 256
FEATURES = 16


def matmul(left, right):
    return jnp.dot(left, right, preferred_element_type=F32)


def matmul_nt(left, right, precision=None):
    return lax.dot_general(
        left, right, (((1,), (1,)), ((), ())), precision=precision, preferred_element_type=F32
    )


def cell_features(plan_ref, depth_ref):
    east = plan_ref[0:1, :] - 128
    north = plan_ref[1:2, :] - 128
    down = depth_ref[...] + 1
    square = east * east + north * north + down * down
    high = (square >> 8) << 8
    low = square & 255
    one = jnp.ones_like(square)
    zero = jnp.zeros_like(square)
    rows = [high, low, one, one, east, north, zero, zero]
    rows += [east, north, one, one, one, zero, zero, zero]
    return jnp.concatenate([row.astype(F32) for row in rows], axis=0)


def station_features(index_ref):
    east, north = index_ref[0:1, :], index_ref[1:2, :]
    whole_e, whole_n = (east >> 8) - 128, (north >> 8) - 128
    part_e, part_n = (east & 255) - 128, (north & 255) - 128
    square = whole_e * whole_e + whole_n * whole_n
    cross = 512 * (whole_e * part_e + whole_n * part_n) + part_e * part_e + part_n * part_n
    one = jnp.ones_like(square).astype(F32)
    zero = jnp.zeros_like(one)
    rows = [
        one,
        one,
        ((square >> 8) << 8).astype(F32),
        (square & 255).astype(F32),
        (-2 * whole_e).astype(F32),
        (-2 * whole_n).astype(F32),
        zero,
        zero,
        part_e.astype(F32) * (-2.0 / 256),
        part_n.astype(F32) * (-2.0 / 256),
        (cross >> 16).astype(F32),
        ((cross >> 8) & 255).astype(F32) * (1.0 / 256),
        (cross & 255).astype(F32) * (1.0 / 65536),
        zero,
        zero,
        zero,
    ]
    return jnp.concatenate(rows, axis=0)


def kernel(
    n_cells,
    n_stations,
    probes_ref,
    reg_ref,
    plan_ref,
    depth_ref,
    index_ref,
    weight_ref,
    image_ref,
    gram_ref,
    sens,
    cell_feat,
    station_feat,
    scale,
    running,
    field_out,
    field_in,
    weighted,
    image_out,
    image_in,
    gram_s,
    gram_c,
    field_send,
    field_recv,
    weighted_send,
    weighted_recv,
    image_send,
    image_recv,
    gs_send,
    gs_recv,
    gc_send,
    gc_recv,
):
    k_rows, cells = probes_ref.shape
    stations = index_ref.shape[1]
    own = stations // n_cells
    quarter = cells // n_stations
    block = max(own, 512)
    block_owners = block // own
    blocks = stations // block
    me_c = lax.axis_index("cells")
    me_s = lax.axis_index("stations")

    def peer_c(step):
        return lax.rem(me_c + step, n_cells)

    def peer_s(step):
        return lax.rem(me_s + step, n_stations)

    barrier = pltpu.get_barrier_semaphore()

    def greet_c(step, carry):
        pl.semaphore_signal(barrier, inc=1, device_id={"cells": peer_c(step)}, device_id_type=MESH)
        return carry

    lax.fori_loop(1, n_cells, greet_c, 0)
    for step in range(1, n_stations):
        pl.semaphore_signal(
            barrier, inc=1, device_id={"stations": peer_s(step)}, device_id_type=MESH
        )

    def field_copy(dest):
        return pltpu.make_async_remote_copy(
            src_ref=field_out.at[dest],
            dst_ref=field_in.at[me_c],
            send_sem=field_send.at[dest],
            recv_sem=field_recv.at[me_c],
            device_id={"cells": dest},
            device_id_type=MESH,
        )

    def field_arrival(source):
        return pltpu.make_async_remote_copy(
            src_ref=field_out.at[source],
            dst_ref=field_in.at[source],
            send_sem=field_send.at[source],
            recv_sem=field_recv.at[source],
            device_id={"cells": source},
            device_id_type=MESH,
        )

    def weighted_copy(dest, source):
        return pltpu.make_async_remote_copy(
            src_ref=weighted.at[source],
            dst_ref=weighted.at[source],
            send_sem=weighted_send.at[dest],
            recv_sem=weighted_recv.at[source],
            device_id={"cells": dest},
            device_id_type=MESH,
        )

    def image_copy(dest, source):
        return pltpu.make_async_remote_copy(
            src_ref=image_out.at[dest],
            dst_ref=image_in.at[source],
            send_sem=image_send.at[dest],
            recv_sem=image_recv.at[source],
            device_id={"stations": dest},
            device_id_type=MESH,
        )

    def gs_copy(dest, source):
        return pltpu.make_async_remote_copy(
            src_ref=gram_s.at[source],
            dst_ref=gram_s.at[source],
            send_sem=gs_send.at[dest],
            recv_sem=gs_recv.at[source],
            device_id={"stations": dest},
            device_id_type=MESH,
        )

    def gc_copy(dest, source):
        return pltpu.make_async_remote_copy(
            src_ref=gram_c.at[source],
            dst_ref=gram_c.at[source],
            send_sem=gc_send.at[dest],
            recv_sem=gc_recv.at[source],
            device_id={"cells": dest},
            device_id_type=MESH,
        )

    cell_feat[...] = cell_features(plan_ref, depth_ref).astype(BF16)
    scale[...] = (depth_ref[...].astype(F32) + 1.0) * 2.0
    features = station_features(index_ref)
    station_feat[...] = features.T.astype(BF16)

    own_block = me_c // block_owners
    width = math.gcd(cells, 8 * TILE)
    chunks = cells // width
    pieces = block // TILE

    def place(turn):
        index = lax.rem(own_block + 1 + turn // chunks, blocks)
        return index, pl.multiple_of(index * block, block), lax.rem(turn, chunks)

    def make_tiles(turn):
        _, start, chunk = place(turn)
        for step in range(width // TILE):
            columns = pl.ds(pl.multiple_of(chunk * width + step * TILE, TILE), TILE)
            factor2 = scale[:, columns]
            rows = pl.ds(start, block)
            distance = matmul(station_feat[rows, :], cell_feat[:, columns])
            inverse = lax.rsqrt(distance)
            sens[rows, columns] = (factor2 * inverse * inverse * inverse).astype(BF16)

    def use_tiles(turn):
        _, start, chunk = place(turn)
        columns = pl.ds(pl.multiple_of(chunk * width, width), width)
        vectors = probes_ref[:, columns]
        for piece in range(pieces):
            rows = pl.ds(start + piece * TILE, TILE)
            into = pl.ds(piece * TILE, TILE)
            before = jnp.where(chunk == 0, 0.0, running[:, into])
            running[:, into] = before + matmul_nt(vectors, sens[rows, columns])

    def send_field(turn):
        index, start, chunk = place(turn)

        @pl.when(chunk == chunks - 1)
        def _():
            station_scale = weight_ref[:, pl.ds(start, block)]
            field = running[...] * (station_scale * station_scale)
            for part in range(block_owners):
                dest = index * block_owners + part
                field_out[dest] = field[:, part * own : (part + 1) * own]

                @pl.when(dest != me_c)
                def _():
                    field_copy(dest).start()

    running[...] = jnp.zeros_like(running)
    make_tiles(0)
    pl.semaphore_wait(barrier, n_cells - 1 + n_stations - 1)

    def forward(turn, carry):
        use_tiles(turn - 1)
        make_tiles(turn)
        send_field(turn - 1)
        return carry

    lax.fori_loop(1, blocks * chunks, forward, 0)
    use_tiles(blocks * chunks - 1)
    send_field(blocks * chunks - 1)

    def add_field(step, before):
        source = peer_c(step)
        field_arrival(source).wait_recv()
        return before + field_in[source]

    total = lax.fori_loop(1, n_cells, add_field, field_out[me_c])
    weighted[me_c] = total.astype(BF16)

    def send_weighted(step, carry):
        weighted_copy(peer_c(step), me_c).start()
        return carry

    lax.fori_loop(1, n_cells, send_weighted, 0)

    def await_weighted(step, carry):
        weighted_copy(peer_c(step), peer_c(step)).wait_recv()
        return carry

    lax.fori_loop(1, n_cells, await_weighted, 0)

    offsets = [2, 1, 3, 0] if n_stations == 4 else list(range(n_stations - 1, -1, -1))
    image = None
    for offset in offsets:
        dest = peer_s(offset)
        columns = pl.ds(pl.multiple_of(dest * quarter, quarter), quarter)

        def backward(step, before):
            rows = pl.ds(pl.multiple_of(step * own, own), own)
            return before + matmul(weighted[step], sens[rows, columns])

        partial = lax.fori_loop(0, n_cells, backward, jnp.zeros((k_rows, quarter), F32), unroll=4)
        if offset:
            image_out[dest] = partial
            image_copy(dest, me_s).start()
        else:
            image = partial + reg_ref[:, columns] * probes_ref[:, columns].astype(F32)

    for step in range(1, n_stations):
        source = peer_s(step)
        image_copy(source, source).wait_recv()
        image = image + image_in[source]

    gram = matmul_nt(image, image, lax.Precision.HIGHEST)
    gram_s[me_s] = gram
    for step in range(1, n_stations):
        gs_copy(peer_s(step), me_s).start()
    for step in range(1, n_stations):
        gs_copy(peer_s(step), peer_s(step)).wait_recv()
    gram = gram_s[0]
    for source in range(1, n_stations):
        gram = gram + gram_s[source]
    gram_c[me_c] = gram

    def send_gram(step, carry):
        gc_copy(peer_c(step), me_c).start()
        return carry

    def await_gram(step, carry):
        gc_copy(peer_c(step), peer_c(step)).wait_recv()
        return carry

    lax.fori_loop(1, n_cells, send_gram, 0)
    lax.fori_loop(1, n_cells, await_gram, 0)
    gram = lax.fori_loop(1, n_cells, lambda s, r: r + gram_c[s], gram_c[0])

    image_ref[...] = image
    gram_ref[...] = gram / (cells * n_cells)

    def finish_c(step, carry):
        dest = peer_c(step)
        field_copy(dest).wait_send()
        weighted_copy(dest, me_c).wait_send()
        gc_copy(dest, me_c).wait_send()
        return carry

    lax.fori_loop(1, n_cells, finish_c, 0)
    for step in range(1, n_stations):
        dest = peer_s(step)
        image_copy(dest, me_s).wait_send()
        gs_copy(dest, me_s).wait_send()


def orthonormalize(image_ref, gram_ref, basis_ref, factor_ref):
    k_rows = image_ref.shape[0]
    image = image_ref[...]
    row = lax.broadcasted_iota(jnp.int32, (k_rows, k_rows), 0)
    col = lax.broadcasted_iota(jnp.int32, (k_rows, k_rows), 1)
    left = gram_ref[...] + jnp.where(row == col, JITTER, 0.0)
    lower = jnp.zeros_like(left)
    row1 = row[:, 0:1]
    for j in range(k_rows):
        pivot = left[j : j + 1, j : j + 1]
        column = left[:, j : j + 1]
        lower = jnp.where((col == j) & (row >= j), column * lax.rsqrt(pivot), lower)
        ratio = jnp.where(row1 > j, column / pivot, 0.0)
        left = left - ratio * left[j : j + 1, :]
        image = image - ratio * image[j : j + 1, :]
    diagonal = jnp.sum(jnp.where(row == col, left, 0.0), axis=1, keepdims=True)
    basis_ref[...] = image * lax.rsqrt(diagonal)
    factor_ref[...] = lower


def body(n_cells, n_stations, probes, reg_weight, cell_plan, cell_depth, station_index, station_weight):
    k_rows, cells = probes.shape
    stations = station_index.shape[1]
    own = stations // n_cells
    quarter = cells // n_stations
    dma = pltpu.SemaphoreType.DMA
    shapes = (
        jax.ShapeDtypeStruct((k_rows, quarter), F32),
        jax.ShapeDtypeStruct((k_rows, k_rows), F32),
    )
    image, gram = pl.pallas_call(
        functools.partial(kernel, n_cells, n_stations),
        out_shape=shapes,
        in_specs=[pl.BlockSpec(memory_space=pltpu.VMEM)] * 6,
        out_specs=(pl.BlockSpec(memory_space=pltpu.VMEM),) * 2,
        scratch_shapes=[
            pltpu.VMEM((stations, cells), BF16),
            pltpu.VMEM((FEATURES, cells), BF16),
            pltpu.VMEM((stations, FEATURES), BF16),
            pltpu.VMEM((1, cells), F32),
            pltpu.VMEM((k_rows, max(own, 512)), F32),
            pltpu.VMEM((n_cells, k_rows, own), F32),
            pltpu.VMEM((n_cells, k_rows, own), F32),
            pltpu.VMEM((n_cells, k_rows, own), BF16),
            pltpu.VMEM((n_stations, k_rows, quarter), F32),
            pltpu.VMEM((n_stations, k_rows, quarter), F32),
            pltpu.VMEM((n_stations, k_rows, k_rows), F32),
            pltpu.VMEM((n_cells, k_rows, k_rows), F32),
            dma((n_cells,)),
            dma((n_cells,)),
            dma((n_cells,)),
            dma((n_cells,)),
            dma((n_stations,)),
            dma((n_stations,)),
            dma((n_stations,)),
            dma((n_stations,)),
            dma((n_cells,)),
            dma((n_cells,)),
        ],
        compiler_params=pltpu.CompilerParams(
            collective_id=0, has_side_effects=True, vmem_limit_bytes=56 * 1024 * 1024
        ),
    )(
        probes,
        reg_weight.reshape(1, -1),
        cell_plan,
        cell_depth.reshape(1, -1),
        station_index,
        station_weight.reshape(1, -1),
    )
    return pl.pallas_call(orthonormalize, out_shape=shapes)(image, gram)


def solution(mesh):
    return jax.shard_map(
        functools.partial(body, mesh.shape["cells"], mesh.shape["stations"]),
        mesh=mesh,
        in_specs=(
            P(None, "cells"),
            P("cells"),
            P(None, "cells"),
            P("cells"),
            P(None, "stations"),
            P("stations"),
        ),
        out_specs=(P(None, ("cells", "stations")), P()),
        check_vma=False,
    )
```
